128 devices in a mesh: slab: 8 (over z, core), tile: 16 (over y, x).
Axes of the slice: x: 4, y: 4, z: 4, core: 2. Of those that a mesh axis runs over, the one named last changes fastest.
Arguments:
- adjoint: float32 [128, 1024, 1024], P('slab', 'tile'), may hold values from -6 to 6
- adjoint_prev: float32 [128, 1024, 1024], P('slab', 'tile'), may hold values from -6 to 6
- courant: float32 [128, 1024, 1024], P('slab', 'tile'), may hold values from 0.15 to 0.5
- wall_cell: int32 [262144], P(('slab', 'tile')), may hold values from 0 to 1048575
- wall_patch: int32 [262144], P(('slab', 'tile')), may hold values from 0 to 4095, as said below
- block_count: int32 [2048], P(('slab', 'tile')), may hold values from 1 to 128, as said below
- wall_damp: float32 [262144], P(('slab', 'tile')), may hold values from 0.1 to 0.6
- history: bfloat16 [3, 262144, 256], P(None, ('slab', 'tile')), may hold values from -1.1953125 to 1.1953125
Outputs:
- patch_gradient: float32 [4096, 256], P('tile')
- final_adjoint: float32 [128, 1024, 1024], P('slab', 'tile')
- previous_adjoint: float32 [128, 1024, 1024], P('slab', 'tile')
The draws below stay inside these ranges and needn't reach their ends.
Inputs may be any that keep to these rules, and one draw needn't show every extreme that they name: `wall_patch`: A slot in block j (slots j * 128 to (j + 1) * 128 - 1 of its device) names a patch from j * (256) to (j + 1) * 256 - 1, whether live or not. `block_count`: in every draw one owner tile gets 128 live slots from every device.
All inputs are finite; a program needn't handle non-finite values.
Results may differ from the reference program's by a relative error of at most 0.0029.
Values may be sent and summed in bfloat16 or wider, within the bound.
A program may use at most 128 MiB of HBM per device.

```python
import math
import jax
import jax.numpy as jnp

CZ = 16
CY = 64
NX = 1024
K = 256
PATCHES = 4096
CAP = 128
STEPS = 3
SLABS = 8
TILES = 16
SLOTS = 2048
ROWS_ALL = 262144
NZ = 128
NY = 1024


def draw_wall_patch(key, part):
    key = jax.random.fold_in(key, 2)
    per_owner = PATCHES // TILES
    slot = jnp.arange(ROWS_ALL, dtype=jnp.int32) % SLOTS
    owner = slot // CAP
    offset = jax.random.randint(key, (ROWS_ALL,), 0, per_owner, dtype=jnp.int32)
    return (owner * per_owner + offset).astype(jnp.int32)


def draw_block_count(key, part):
    key = jax.random.fold_in(key, 3)
    first_key, second_key = jax.random.split(key)
    full_owner = jax.random.randint(first_key, (), 0, TILES, dtype=jnp.int32)
    counts = jax.random.randint(second_key, (SLABS * TILES, TILES), 1, CAP + 1, dtype=jnp.int32)
    owner = jnp.arange(TILES, dtype=jnp.int32)[None, :]
    counts = jnp.where(owner == full_owner, CAP, counts)
    return counts.reshape(-1).astype(jnp.int32)


def touch_ends(drawn, key, low, high):
    shape = drawn.shape
    place = [jax.random.randint(jax.random.fold_in(key, axis), (), 0, shape[axis]) for axis in range(len(shape))]
    drawn = drawn.at[tuple(place)].set(low)
    longest = shape.index(max(shape))
    place[longest] = (place[longest] + 1) % shape[longest]
    return drawn.at[tuple(place)].set(high)


def level_of(key, shape, pieces, least, high):
    level, own = 1.0, jax.random.fold_in(key, 6)
    for dim, parts in pieces:
        heights = jnp.exp(jax.random.uniform(jax.random.fold_in(own, dim), (parts,), jnp.float32, least / len(pieces), high / len(pieces)))
        level = level * jnp.repeat(heights, shape[dim] // parts).reshape([-1 if axis == dim else 1 for axis in range(len(shape))])
    return level


def gaussian(key, extent, width, reach, cuts=(), kind=jnp.bfloat16):
    entries = width * jax.random.normal(key, extent, jnp.float32)
    if cuts:
        entries = entries * level_of(key, extent, cuts, -0.22, 0.18)
    return jnp.clip(entries, -reach, reach).astype(kind)


def setup_inputs(seed: int = 0) -> dict:
    splits = jax.random.split(jax.random.key(seed), 9)
    adjoint = gaussian(splits[0], (NZ, NY, NX), 1.0, 6.0, ((0, 8), (1, 16)), jnp.float32)
    adjoint_prev = gaussian(splits[1], (NZ, NY, NX), 1.0, 6.0, ((0, 8), (1, 16)), jnp.float32)
    courant = jnp.clip(jnp.exp(math.log(0.5) - 1.2039728 * jax.random.uniform(splits[2], (NZ, NY, NX), jnp.float32) ** level_of(splits[2], (NZ, NY, NX), ((0, 8), (1, 16)), -0.2, 0.2)), 0.15, 0.5)
    wall_cell = touch_ends(jax.random.randint(splits[3], (ROWS_ALL,), 0, CZ * CY * NX), jax.random.fold_in(splits[3], 1), 0, (CZ * CY * NX) - 1).astype(jnp.int32)
    wall_patch = draw_wall_patch(jax.random.fold_in(splits[8], 71), 0)
    block_count = draw_block_count(jax.random.fold_in(splits[8], 71), 0)
    wall_damp = jnp.clip(0.1 + 0.5 * jax.random.uniform(splits[6], (ROWS_ALL,), jnp.float32) ** level_of(splits[6], (ROWS_ALL,), ((0, 128),), -0.2, 0.2), 0.1, 0.6)
    history = gaussian(splits[7], (STEPS, ROWS_ALL, K), 0.2, 1.1953125, ((1, 128),))
    return dict(adjoint=adjoint, adjoint_prev=adjoint_prev, courant=courant, wall_cell=wall_cell, wall_patch=wall_patch, block_count=block_count, wall_damp=wall_damp, history=history)


face_weight = 0.5
edge_weight = 0.125
corner_weight = 0.0625


def stencil(padded):
    mid_x = padded[:, :, 1:-1]
    side_x = padded[:, :, :-2] + padded[:, :, 2:]
    mid_mid = mid_x[:, 1:-1]
    mid_side = mid_x[:, :-2] + mid_x[:, 2:]
    side_mid = side_x[:, 1:-1]
    side_side = side_x[:, :-2] + side_x[:, 2:]
    center = mid_mid[1:-1]
    face_z = mid_mid[:-2] + mid_mid[2:]
    faces = face_z + mid_side[1:-1] + side_mid[1:-1]
    edges = (mid_side[:-2] + mid_side[2:]) + (side_mid[:-2] + side_mid[2:]) + side_side[1:-1]
    corners = side_side[:-2] + side_side[2:]
    return face_weight * faces + edge_weight * edges + corner_weight * corners - 5.0 * center


def reference(adjoint, adjoint_prev, courant, wall_cell, wall_patch, block_count, wall_damp, history):
    rows = jnp.arange(ROWS_ALL, dtype=jnp.int32)
    device = rows // SLOTS
    slot = rows % SLOTS
    slab_index = device // TILES
    tile_index = device % TILES
    cell_z = wall_cell // (CY * NX)
    cell_y = (wall_cell // NX) % CY
    cell_x = wall_cell % NX
    global_cell = (((slab_index * CZ + cell_z) * NY + tile_index * CY + cell_y) * NX + cell_x).astype(jnp.int32)
    counts = block_count.reshape(SLABS * TILES, TILES)
    limit = counts[device, slot // CAP]
    live = ((slot % CAP) < limit).astype(jnp.float32)
    coeff = wall_damp * live
    shape = adjoint.shape
    lam = adjoint
    prev = adjoint_prev
    acc = jnp.zeros((ROWS_ALL, K), jnp.float32)
    for step in range(STEPS):
        laplace = stencil(jnp.pad(lam, 1))
        following = 2.0 * lam - prev + courant * laplace
        lam_flat = lam.reshape(-1)
        prev_flat = prev.reshape(-1)
        change = -coeff * (lam_flat[global_cell] - prev_flat[global_cell])
        flat = following.reshape(-1).at[global_cell].add(change)
        acc = acc + flat[global_cell][:, None] * history[step].astype(jnp.float32)
        prev = lam
        lam = flat.reshape(shape)
    wall_rows = (acc * live[:, None]).astype(jnp.bfloat16)
    gradient = jnp.zeros((PATCHES, K), jnp.float32).at[wall_patch].add(wall_rows.astype(jnp.float32))
    return gradient, lam, prev
```

```python
import jax
import jax.numpy as jnp
from jax import lax
from jax.experimental import pallas as pl
from jax.experimental.pallas import tpu as pltpu
from jax.sharding import PartitionSpec as P

PATCHES = 4096
CZ, CY, NX, LANES = 16, 64, 1024, 128
SUB = NX // LANES
SLOTS, K, STEPS = 2048, 256, 3
SLABS, TILES = 8, 16
CAP = SLOTS // TILES
OWN = PATCHES // TILES
MESH = pl.DeviceIdType.MESH
MIB = 1 << 20
NT = (((1,), (1,)), ((), ()))
DIRS = [(-1, 0), (1, 0), (-1, -1), (-1, 1), (1, -1), (1, 1), (0, -1), (0, 1)]


def damp_kernel(cell_s, count_s, cell_v, damp_v, keep, inc, old):
    def clear(i, carry):
        keep[pl.ds(pl.multiple_of(i * 64, 64), 64), :] = jnp.ones((64, LANES), jnp.float32)
        return carry

    lax.fori_loop(0, CZ * CY * SUB // 64, clear, 0)
    shape = (CAP, LANES)

    def block(j, carry):
        cell = cell_v[pl.ds(j, 1), :]
        damp = damp_v[pl.ds(j, 1), :]
        live = lax.broadcasted_iota(jnp.int32, (1, CAP), 1) < count_s[j]
        damp = jnp.where(live, damp, 0.0)
        row = jnp.broadcast_to((cell >> 7).astype(jnp.float32), shape)
        lane = jnp.broadcast_to(cell & 127, shape)
        same = jnp.where(row.T == row, jnp.broadcast_to(damp, shape), 0.0)
        onehot = (lane == lax.broadcasted_iota(jnp.int32, shape, 0)).astype(jnp.bfloat16)
        high = same.astype(jnp.bfloat16)
        rest = same - high.astype(jnp.float32)
        mid = rest.astype(jnp.bfloat16)
        low = (rest - mid.astype(jnp.float32)).astype(jnp.bfloat16)

        def place(part):
            return lax.dot_general(part, onehot, NT, preferred_element_type=jnp.float32)

        inc[...] = place(high) + place(mid) + place(low)
        base = pl.multiple_of(j * CAP, CAP)
        for k in range(CAP):
            old[pl.ds(k, 1), :] = keep[pl.ds(cell_s[base + k] >> 7, 1), :]
        inc[...] = old[...] - inc[...]
        for k in range(CAP):
            keep[pl.ds(cell_s[base + k] >> 7, 1), :] = inc[pl.ds(k, 1), :]
        return carry

    lax.fori_loop(0, TILES, block, 0)


def steps_kernel(
    adjoint, adjoint_prev, courant, keep, lam1, lam2, lam3,
    lam0, before, cour, load_sem, send_sem, recv_sem,
):
    slab, tile = lax.axis_index("slab"), lax.axis_index("tile")

    def chunk(src, dst, sem):
        for s in range(SUB):
            pltpu.make_async_copy(src.at[:, :, pl.ds(s * LANES, LANES)], dst.at[:, :, s, :], sem).start()

    inner = lam0.at[pl.ds(1, CZ), pl.ds(1, CY)]
    chunk(adjoint, inner, load_sem.at[0])
    chunk(adjoint_prev, before, load_sem.at[1])
    chunk(courant, cour, load_sem.at[2])

    def has(dz, dy):
        z, y = slab + dz, tile + dy
        return (z >= 0) & (z < SLABS) & (y >= 0) & (y < TILES)

    barrier = pltpu.get_barrier_semaphore()
    for dz, dy in DIRS:
        @pl.when(has(dz, dy))
        def _():
            pl.semaphore_signal(barrier, inc=1, device_id=(slab + dz, tile + dy), device_id_type=MESH)
    zs = jnp.where((slab == 0) | (slab == SLABS - 1), 2, 3)
    ys = jnp.where((tile == 0) | (tile == TILES - 1), 2, 3)

    for lam in (lam0, lam1, lam2):
        for at, there in ((0, slab == 0), (CZ + 1, slab == SLABS - 1)):
            @pl.when(there)
            def _():
                lam[at] = jnp.zeros((CY + 2, SUB, LANES), jnp.float32)
        for at, there in ((0, tile == 0), (CY + 1, tile == TILES - 1)):
            @pl.when(there)
            def _():
                for z in range(CZ + 2):
                    lam[z, at] = jnp.zeros((SUB, LANES), jnp.float32)
    pl.semaphore_wait(barrier, zs * ys - 1)

    def message(n, d):
        lam = (lam0, lam1, lam2)[n]
        dz, dy = DIRS[d]
        src_z = {-1: 1, 0: pl.ds(1, CZ), 1: CZ}[dz]
        dst_z = {-1: CZ + 1, 0: pl.ds(1, CZ), 1: 0}[dz]
        src_y = {-1: 1, 0: pl.ds(1, CY), 1: CY}[dy]
        dst_y = {-1: CY + 1, 0: pl.ds(1, CY), 1: 0}[dy]
        return pltpu.make_async_remote_copy(
            src_ref=lam.at[src_z, src_y],
            dst_ref=lam.at[dst_z, dst_y],
            send_sem=send_sem.at[n, d],
            recv_sem=recv_sem.at[n, d],
            device_id=(slab + dz, tile + dy),
            device_id_type=MESH,
        )

    def send(n, which):
        for d in which:
            @pl.when(has(*DIRS[d]))
            def _():
                message(n, d).start()

    def receive(n):
        for d in range(8):
            dz, dy = DIRS[d]
            @pl.when(has(-dz, -dy))
            def _():
                message(n, d).wait_recv()

    lane = lax.broadcasted_iota(jnp.int32, (SUB, LANES), 1)
    sub = lax.broadcasted_iota(jnp.int32, (SUB, LANES), 0)
    first_lane, last_lane = lane == 0, lane == LANES - 1
    not_first = jnp.where(sub == 0, 0.0, 1.0)
    not_last = jnp.where(sub == SUB - 1, 0.0, 1.0)

    def x_sides(q):
        left = pltpu.roll(q, 1, 1)
        right = pltpu.roll(q, LANES - 1, 1)
        left = jnp.where(first_lane, pltpu.roll(left, 1, 0) * not_first, left)
        right = jnp.where(last_lane, pltpu.roll(right, SUB - 1, 0) * not_last, right)
        return left + right

    def rows(n, z, first, count):
        lam = (lam0, lam1, lam2)[n]

        def parts(y):
            mid = lam[z, y]
            sides = lam[z - 1, y] + lam[z + 1, y]
            quarter = sides * 0.25
            a = mid + quarter
            b = (a + quarter) * 0.25
            return mid, sides, a, b

        down, here = parts(first - 1), parts(first)
        for k in range(count):
            y = first + k
            up = parts(y + 1)
            mid, sides, a, b = here
            q = a + (down[3] + up[3])
            twice = (sides - 10.0 * mid) + (down[2] + up[2]) + x_sides(q)
            prev = before[z - 1, y - 1] if n == 0 else (lam0, lam1)[n - 1][z, y]
            new = mid + (mid - prev) * keep[z - 1, y - 1] + cour[z - 1, y - 1] * (0.5 * twice)
            if n == 2:
                lam3[z - 1, y - 1] = new
            else:
                (lam1, lam2)[n][z, y] = new
            down, here = here, up

    half = (CY - 2) // 2

    def step(n):
        def inside(i, carry):
            rows(n, 2 + i // 2, 2 + (i % 2) * half, half)
            return carry

        lax.fori_loop(0, 2 * (CZ - 2), inside, 0)
        receive(n)

        def layer(i, carry):
            rows(n, 1 + (i // 2) * (CZ - 1), 1 + (i % 2) * (CY // 2), CY // 2)
            return carry

        lax.fori_loop(0, 4, layer, 0)
        if n < 2:
            send(n + 1, range(6))

        def edge(i, carry):
            rows(n, 2 + i, 1, 1)
            rows(n, 2 + i, CY, 1)
            return carry

        lax.fori_loop(0, CZ - 2, edge, 0)
        if n < 2:
            send(n + 1, range(6, 8))

    pltpu.make_async_copy(inner, inner, load_sem.at[0]).wait()
    send(0, range(8))
    pltpu.make_async_copy(before, before, load_sem.at[1]).wait()
    pltpu.make_async_copy(cour, cour, load_sem.at[2]).wait()
    for n in range(STEPS):
        step(n)
    for n in range(STEPS):
        for d in range(8):
            @pl.when(has(*DIRS[d]))
            def _():
                message(n, d).wait_send()


def rows_kernel(
    cell_s, count_s, cell_v, lam1, lam2, lam3, lam2_full, lam3_full, history,
    rows, final, previous, hist, got, out_sem, hist_sem,
):
    inner = lam2_full.at[pl.ds(1, CZ), pl.ds(1, CY)]
    copies = []
    for n in range(STEPS):
        pltpu.make_async_copy(history.at[n], hist.at[n], hist_sem.at[n]).start()
    for src, dst, sem in ((inner, previous, 0), (lam3_full, final, 1)):
        for s in range(SUB):
            copy = pltpu.make_async_copy(
                src.at[:, :, s, :], dst.at[:, :, pl.ds(s * LANES, LANES)], out_sem.at[sem, s]
            )
            copy.start()
            copies.append(copy)
    for n in range(STEPS):
        pltpu.make_async_copy(history.at[n], hist.at[n], hist_sem.at[n]).wait()
    shape = (CAP, LANES)

    def block(j, carry):
        base = pl.multiple_of(j * CAP, CAP)
        for k in range(CAP):
            cell = cell_s[base + k]
            flat = cell >> 7
            padded = flat + ((cell >> 16) << 4) + (CY + 3) * SUB
            got[0, pl.ds(k, 1), :] = lam1[pl.ds(padded, 1), :]
            got[1, pl.ds(k, 1), :] = lam2[pl.ds(padded, 1), :]
            got[2, pl.ds(k, 1), :] = lam3[pl.ds(flat, 1), :]
        lane = jnp.broadcast_to((cell_v[pl.ds(j, 1), :] & 127).astype(jnp.float32), shape).T
        here = lane.astype(jnp.int32) == lax.broadcasted_iota(jnp.int32, shape, 1)
        acc = jnp.zeros((CAP, K), jnp.float32)
        for n in range(STEPS):
            value = jnp.sum(jnp.where(here, got[n], 0.0), axis=1, keepdims=True)
            acc = acc + value * hist[n, pl.ds(base, CAP), :].astype(jnp.float32)
        live = lax.broadcasted_iota(jnp.int32, (CAP, K), 0) < count_s[j]
        rows[j] = jnp.where(live, acc, 0.0).astype(jnp.bfloat16)
        return carry

    lax.fori_loop(0, TILES, block, 0)
    for copy in copies:
        copy.wait()


def patch_kernel(
    rows, ids, out, got_rows, got_ids, total, chunks, result,
    id_send, id_recv, row_send, row_recv, part_send, part_recv, all_send, all_recv,
):
    slab, tile = lax.axis_index("slab"), lax.axis_index("tile")
    barrier = pltpu.get_barrier_semaphore()
    for k in range(1, TILES):
        pl.semaphore_signal(barrier, inc=1, device_id=(slab, (tile + k) % TILES), device_id_type=MESH)
    for k in range(1, SLABS):
        pl.semaphore_signal(barrier, inc=1, device_id=((slab + k) % SLABS, tile), device_id_type=MESH)
    pl.semaphore_wait(barrier, TILES + SLABS - 2)

    def to_tile(src, dst, send_sem, recv_sem, k):
        owner = (tile + k) % TILES
        return pltpu.make_async_remote_copy(
            src_ref=src.at[owner], dst_ref=dst.at[k], send_sem=send_sem.at[k], recv_sem=recv_sem.at[k],
            device_id=(slab, owner), device_id_type=MESH,
        )

    for k in range(1, TILES):
        to_tile(ids, got_ids, id_send, id_recv, k).start()
    for k in range(1, TILES):
        to_tile(rows, got_rows, row_send, row_recv, k).start()

    def summed(named, block):
        local = named - tile * OWN
        onehot = (
            jnp.broadcast_to(local, (OWN, CAP)) == lax.broadcasted_iota(jnp.int32, (OWN, CAP), 0)
        ).astype(jnp.bfloat16)
        return jnp.dot(onehot, block, preferred_element_type=jnp.float32)

    total[...] = summed(ids[tile], rows[tile])
    for k in range(1, TILES):
        to_tile(ids, got_ids, id_send, id_recv, k).wait_recv()
        to_tile(rows, got_rows, row_send, row_recv, k).wait_recv()
        total[...] += summed(got_ids[k], got_rows[k])

    part = OWN // SLABS
    mine = pl.ds(pl.multiple_of(slab * part, part), part)

    def to_slab(k):
        owner = (slab + k) % SLABS
        return pltpu.make_async_remote_copy(
            src_ref=total.at[pl.ds(pl.multiple_of(owner * part, part), part)], dst_ref=chunks.at[k],
            send_sem=part_send.at[k], recv_sem=part_recv.at[k], device_id=(owner, tile), device_id_type=MESH,
        )

    def to_all(k):
        return pltpu.make_async_remote_copy(
            src_ref=result.at[mine], dst_ref=result.at[mine],
            send_sem=all_send.at[k], recv_sem=all_recv.at[k],
            device_id=((slab + k) % SLABS, tile), device_id_type=MESH,
        )

    def from_all(k):
        owner = (slab + SLABS - k) % SLABS
        theirs = pl.ds(pl.multiple_of(owner * part, part), part)
        return pltpu.make_async_remote_copy(
            src_ref=result.at[mine], dst_ref=result.at[theirs],
            send_sem=all_send.at[k], recv_sem=all_recv.at[k],
            device_id=((slab + k) % SLABS, tile), device_id_type=MESH,
        )

    for k in range(1, SLABS):
        to_slab(k).start()
    mean = total[mine, :]
    for k in range(1, SLABS):
        to_slab(k).wait_recv()
        mean = mean + chunks[k]
    result[mine, :] = mean
    for k in range(1, SLABS):
        to_all(k).start()
    for k in range(1, SLABS):
        from_all(k).wait_recv()
    out[...] = result[...]
    for k in range(1, TILES):
        to_tile(ids, got_ids, id_send, id_recv, k).wait_send()
        to_tile(rows, got_rows, row_send, row_recv, k).wait_send()
    for k in range(1, SLABS):
        to_slab(k).wait_send()
        to_all(k).wait_send()


SMEM = pl.BlockSpec(memory_space=pltpu.SMEM)
VMEM = pl.BlockSpec(memory_space=pltpu.VMEM)
ANY = pl.BlockSpec(memory_space=pl.ANY)
F32, BF16, I32 = jnp.float32, jnp.bfloat16, jnp.int32
DMA = pltpu.SemaphoreType.DMA


def keep_in_vmem(array):
    return pltpu.with_memory_space_constraint(array, pltpu.VMEM)


def on_device(adjoint, adjoint_prev, courant, wall_cell, wall_patch, block_count, wall_damp, history):
    field = (CZ, CY, SUB, LANES)
    padded = (CZ + 2, CY + 2, SUB, LANES)
    cells = wall_cell.reshape(TILES, CAP)
    keep = pl.pallas_call(
        damp_kernel,
        out_shape=pltpu.VMEM((CZ * CY * SUB, LANES), F32),
        in_specs=[SMEM, SMEM, VMEM, VMEM],
        out_specs=VMEM,
        scratch_shapes=[pltpu.VMEM((CAP, LANES), F32)] * 2,
        compiler_params=pltpu.CompilerParams(vmem_limit_bytes=4 * MIB),
        name="damp",
    )(wall_cell, block_count, cells, wall_damp.reshape(TILES, CAP))
    keep = keep.reshape(field)
    lam1, lam2, lam3 = pl.pallas_call(
        steps_kernel,
        out_shape=(pltpu.VMEM(padded, F32), pltpu.VMEM(padded, F32), pltpu.VMEM(field, F32)),
        in_specs=[ANY, ANY, ANY, VMEM],
        out_specs=(VMEM, VMEM, VMEM),
        scratch_shapes=[
            pltpu.VMEM(padded, F32), pltpu.VMEM(field, F32), pltpu.VMEM(field, F32),
            DMA((3,)), DMA((3, 8)), DMA((3, 8)),
        ],
        compiler_params=pltpu.CompilerParams(
            vmem_limit_bytes=18 * MIB, collective_id=0, has_side_effects=True
        ),
        name="steps",
    )(adjoint, adjoint_prev, courant, keep_in_vmem(keep))
    flat1 = lam1.reshape(-1, LANES)
    flat2 = lam2.reshape(-1, LANES)
    flat3 = lam3.reshape(-1, LANES)
    rows, final, previous = pl.pallas_call(
        rows_kernel,
        out_shape=(
            jax.ShapeDtypeStruct((TILES, CAP, K), BF16),
            jax.ShapeDtypeStruct((CZ, CY, NX), F32),
            jax.ShapeDtypeStruct((CZ, CY, NX), F32),
        ),
        in_specs=[SMEM, SMEM, VMEM, VMEM, VMEM, VMEM, VMEM, VMEM, ANY],
        out_specs=(VMEM, ANY, ANY),
        scratch_shapes=[
            pltpu.VMEM((STEPS, SLOTS, K), BF16), pltpu.VMEM((STEPS, CAP, LANES), F32),
            DMA((2, SUB)), DMA((STEPS,)),
        ],
        compiler_params=pltpu.CompilerParams(vmem_limit_bytes=16 * MIB),
        name="rows",
    )(
        wall_cell, block_count, cells, keep_in_vmem(flat1), keep_in_vmem(flat2), keep_in_vmem(flat3),
        keep_in_vmem(lam2), keep_in_vmem(lam3), history,
    )
    part = OWN // SLABS
    gradient = pl.pallas_call(
        patch_kernel,
        out_shape=jax.ShapeDtypeStruct((OWN, K), F32),
        in_specs=[VMEM, VMEM],
        out_specs=VMEM,
        scratch_shapes=[
            pltpu.VMEM((TILES, CAP, K), BF16), pltpu.VMEM((TILES, 1, CAP), I32),
            pltpu.VMEM((OWN, K), F32), pltpu.VMEM((SLABS, part, K), F32), pltpu.VMEM((OWN, K), F32),
            DMA((TILES,)), DMA((TILES,)), DMA((TILES,)), DMA((TILES,)),
            DMA((SLABS,)), DMA((SLABS,)), DMA((SLABS,)), DMA((SLABS,)),
        ],
        compiler_params=pltpu.CompilerParams(
            vmem_limit_bytes=16 * MIB, collective_id=1, has_side_effects=True
        ),
        name="patch",
    )(rows, wall_patch.reshape(TILES, 1, CAP))
    return gradient, final, previous


def solution(mesh):
    return jax.shard_map(
        on_device,
        mesh=mesh,
        in_specs=(
            P("slab", "tile", None),
            P("slab", "tile", None),
            P("slab", "tile", None),
            P(("slab", "tile")),
            P(("slab", "tile")),
            P(("slab", "tile")),
            P(("slab", "tile")),
            P(None, ("slab", "tile"), None),
        ),
        out_specs=(P("tile", None), P("slab", "tile", None), P("slab", "tile", None)),
        check_vma=False,
    )
```

```python
import jax
import jax.numpy as jnp
from jax import lax
from jax.experimental import pallas as pl
from jax.experimental.pallas import tpu as pltpu
from jax.sharding import PartitionSpec as P

PATCHES = 4096
CZ, CY, NX, LANES = 16, 64, 1024, 128
SUB = NX // LANES
FLAT = CZ * CY * SUB
SLOTS, K, STEPS = 2048, 256, 3
SLABS, TILES, SIDE = 8, 16, 4
CAP = SLOTS // TILES
OWN = PATCHES // TILES
HALVES, WIDE = 2, 128
PART = OWN // SLABS
MESH = pl.DeviceIdType.MESH
MIB = 1 << 20
NT = (((1,), (1,)), ((), ()))
DIRS = [(-1, 0), (1, 0), (-1, -1), (-1, 1), (1, -1), (1, 1), (0, -1), (0, 1)]
OFFSETS = sorted(
    range(1, TILES),
    key=lambda k: -min(k // SIDE, SIDE - k // SIDE) - min(k % SIDE, SIDE - k % SIDE),
)
PICKS = SLOTS // CZ
EARLY = 8


def damp_kernel(
    count, cells, damps, adjoint, adjoint_prev, courant,
    keep, lam0, before, cour,
    row_s, count_s, cell_v, damp_v, row_v, inc, old, load_sem, small_sem,
):
    small = [(count, count_s), (cells, cell_v), (damps, damp_v)]
    for i, (src, dst) in enumerate(small):
        pltpu.make_async_copy(src, dst, small_sem.at[i]).start()
    for i, (src, dst) in enumerate(((adjoint, lam0), (adjoint_prev, before), (courant, cour))):
        for s in range(SUB):
            pltpu.make_async_copy(
                src.at[:, :, pl.ds(s * LANES, LANES)], dst.at[:, :, s, :], load_sem.at[i]
            ).start()

    def clear(i, carry):
        keep[pl.ds(pl.multiple_of(i * 128, 128), 128), :] = jnp.ones((128, LANES), jnp.float32)
        return carry

    lax.fori_loop(0, FLAT // 128, clear, 0)
    for i, (src, dst) in enumerate(small):
        pltpu.make_async_copy(src, dst, small_sem.at[i]).wait()
    row_v[...] = cell_v[...] >> 7
    table = pltpu.make_async_copy(row_v, row_s, small_sem.at[3])
    table.start()
    shape = (CAP, LANES)

    def loss(j, carry):
        cell = cell_v[pl.ds(j, 1), :]
        live = lax.broadcasted_iota(jnp.int32, (1, CAP), 1) < count_s[j]
        damp = jnp.where(live, damp_v[pl.ds(j, 1), :], 0.0)
        row = jnp.broadcast_to((cell >> 7).astype(jnp.float32), shape)
        lane = jnp.broadcast_to(cell & 127, shape)
        same = jnp.where(row.T == row, jnp.broadcast_to(damp, shape), 0.0)
        onehot = (lane == lax.broadcasted_iota(jnp.int32, shape, 0)).astype(jnp.bfloat16)
        high = same.astype(jnp.bfloat16)
        rest = same - high.astype(jnp.float32)
        mid = rest.astype(jnp.bfloat16)
        low = (rest - mid.astype(jnp.float32)).astype(jnp.bfloat16)

        def place(part):
            return lax.dot_general(part, onehot, NT, preferred_element_type=jnp.float32)

        inc[pl.ds(pl.multiple_of(j * CAP, CAP), CAP), :] = place(high) + place(mid) + place(low)
        return carry

    lax.fori_loop(0, TILES, loss, 0, unroll=4)
    table.wait()

    def block(j, carry):
        base = pl.multiple_of(j * CAP, CAP)
        for k in range(CAP):
            old[pl.ds(k, 1), :] = keep[pl.ds(row_s[j, k], 1), :]
        old[...] = old[...] - inc[pl.ds(base, CAP), :]
        for k in range(CAP):
            keep[pl.ds(row_s[j, k], 1), :] = old[pl.ds(k, 1), :]
        return carry

    lax.fori_loop(0, TILES, block, 0)
    for i, dst in enumerate((lam0, before, cour)):
        pltpu.make_async_copy(dst, dst, load_sem.at[i]).wait()


def stepper(lam, layer_z, layer_y, before, keep, cour, out, cell_s=None, got=None):
    lane = lax.broadcasted_iota(jnp.int32, (SUB, LANES), 1)
    sub = lax.broadcasted_iota(jnp.int32, (SUB, LANES), 0)
    first_lane, last_lane = lane == 0, lane == LANES - 1
    not_first = jnp.where(sub == 0, 0.0, 1.0)
    not_last = jnp.where(sub == SUB - 1, 0.0, 1.0)
    flat = lam.reshape(FLAT, LANES) if got is not None else None

    def x_sides(q):
        left = pltpu.roll(q, 1, 1)
        right = pltpu.roll(q, LANES - 1, 1)
        left = jnp.where(first_lane, pltpu.roll(left, 1, 0) * not_first, left)
        right = jnp.where(last_lane, pltpu.roll(right, SUB - 1, 0) * not_last, right)
        return left + right

    def cells(z, y):
        if isinstance(z, int) and not 0 <= z < CZ:
            return layer_z[int(z > 0), y + 1]
        if isinstance(y, int) and not 0 <= y < CY:
            return layer_y[int(y > 0), z]
        return lam[z, y]

    def rows(z, first, count, picks=None):
        def parts(y):
            mid = cells(z, y)
            sides = cells(z - 1, y) + cells(z + 1, y)
            quarter = sides * 0.25
            a = mid + quarter
            return mid, sides, a, (a + quarter) * 0.25

        down, here = parts(first - 1), parts(first)
        for k in range(count):
            y = first + k
            up = parts(y + 1)
            mid, sides, a, b = here
            q = a + (down[3] + up[3])
            twice = (sides - 10.0 * mid) + (down[2] + up[2]) + x_sides(q)
            out[z, y] = mid + (mid - before[z, y]) * keep[z, y] + cour[z, y] * (0.5 * twice)
            down, here = here, up
            if got is not None and picks is not None:
                for slot in range(PICKS * k // count, PICKS * (k + 1) // count):
                    at = picks * PICKS + slot
                    got[pl.ds(at, 1), :] = flat[pl.ds(cell_s[at] >> 7, 1), :]

    def inside(first, last):
        def layer(z, carry):
            rows(z, 1, CY - 2, z)
            return carry

        lax.fori_loop(first, last + 1, layer, 0)

    def layers():
        for z in (0, CZ - 1):
            rows(z, 0, CY, z)

    def edges():
        def edge(i, carry):
            for k in range(7):
                rows(1 + 7 * i + k, 0, 1)
                rows(1 + 7 * i + k, CY - 1, 1)
            return carry

        lax.fori_loop(0, (CZ - 2) // 7, edge, 0)

    return inside, layers, edges


def steps_kernel(
    lam0, before, cour, keep, cell,
    lam1, lam2, lam3, last_z, last_y, got1, got2,
    layer_z, layer_y, cell_s, cell_sem, send_sem, recv_sem,
):
    slab, tile = lax.axis_index("slab"), lax.axis_index("tile")

    def has(dz, dy):
        z, y = slab + dz, tile + dy
        return (z >= 0) & (z < SLABS) & (y >= 0) & (y < TILES)

    barrier = pltpu.get_barrier_semaphore()
    for dz, dy in DIRS:
        @pl.when(has(dz, dy))
        def _():
            pl.semaphore_signal(barrier, inc=1, device_id=(slab + dz, tile + dy), device_id_type=MESH)
    zs = jnp.where((slab == 0) | (slab == SLABS - 1), 2, 3)
    ys = jnp.where((tile == 0) | (tile == TILES - 1), 2, 3)
    pltpu.make_async_copy(cell, cell_s, cell_sem).start()
    lams = (lam0, lam1, lam2)
    zlayers = (layer_z.at[0], layer_z.at[1], last_z)
    ylayers = (layer_y.at[0], layer_y.at[1], last_y)

    for n in range(STEPS):
        for side, no_z, no_y in ((0, slab == 0, tile == 0), (1, slab == SLABS - 1, tile == TILES - 1)):
            @pl.when(no_z)
            def _():
                zlayers[n][side] = jnp.zeros((CY + 2, SUB, LANES), jnp.float32)
            @pl.when(no_y)
            def _():
                ylayers[n][side] = jnp.zeros((CZ, SUB, LANES), jnp.float32)
                for z in range(2):
                    zlayers[n][z, side * (CY + 1)] = jnp.zeros((SUB, LANES), jnp.float32)

    def message(n, d):
        dz, dy = DIRS[d]
        src_z = {-1: 0, 0: pl.ds(0, CZ), 1: CZ - 1}[dz]
        src_y = {-1: 0, 0: pl.ds(0, CY), 1: CY - 1}[dy]
        if dz:
            dst = zlayers[n].at[int(dz < 0), {-1: CY + 1, 0: pl.ds(1, CY), 1: 0}[dy]]
        else:
            dst = ylayers[n].at[int(dy < 0)]
        return pltpu.make_async_remote_copy(
            src_ref=lams[n].at[src_z, src_y],
            dst_ref=dst,
            send_sem=send_sem.at[n, d],
            recv_sem=recv_sem.at[n, d],
            device_id=(slab + dz, tile + dy),
            device_id_type=MESH,
        )

    def send(n, which):
        for d in which:
            @pl.when(has(*DIRS[d]))
            def _():
                message(n, d).start()

    def receive(n):
        for d in range(8):
            dz, dy = DIRS[d]
            @pl.when(has(-dz, -dy))
            def _():
                message(n, d).wait_recv()

    first = stepper(lam0, zlayers[0], ylayers[0], before, keep, cour, lam1)
    second = stepper(lam1, zlayers[1], ylayers[1], lam0, keep, cour, lam2, cell_s, got1)
    third = stepper(lam2, zlayers[2], ylayers[2], lam1, keep, cour, lam3, cell_s, got2)

    def outer(n, step):
        receive(n - 1)
        step[1]()
        send(n, range(6))
        step[2]()
        send(n, range(6, 8))

    first[0](1, 5)
    pl.semaphore_wait(barrier, zs * ys - 1)
    send(0, range(8))
    first[0](6, CZ - 2)
    outer(1, first)
    pltpu.make_async_copy(cell, cell_s, cell_sem).wait()
    second[0](1, CZ - 2)
    outer(2, second)
    third[0](1, EARLY)
    receive(2)
    for n in range(STEPS):
        for d in range(8):
            @pl.when(has(*DIRS[d]))
            def _():
                message(n, d).wait_send()


def last_kernel(
    lam1, lam2, begun, begun2, layer_z, layer_y, keep, cour, cell,
    lam3, final, previous, got2,
    cell_s, cell_sem, out_sem,
):
    del begun, begun2

    def writes(src, dst, first, count, sem):
        return [
            pltpu.make_async_copy(
                src.at[pl.ds(first, count), :, s, :],
                dst.at[pl.ds(first, count), :, pl.ds(s * LANES, LANES)],
                out_sem.at[sem, s],
            )
            for s in range(SUB)
        ]

    copies = writes(lam2, previous, 0, CZ, 0)
    pltpu.make_async_copy(cell, cell_s, cell_sem).start()
    for copy in copies:
        copy.start()
    pltpu.make_async_copy(cell, cell_s, cell_sem).wait()
    inside, layers, edges = stepper(lam2, layer_z, layer_y, lam1, keep, cour, lam3, cell_s, got2)

    edges()
    layers()
    done = 1 + EARLY
    head = writes(lam3, final, 0, done, 1)
    for copy in head:
        copy.start()
    inside(done, CZ - 2)
    tail = writes(lam3, final, done, CZ - done, 2)
    for copy in tail:
        copy.start()
    for copy in copies + head + tail:
        copy.wait()


def patch_kernel(
    cell, count, ids, cells, lam3, got1, got2, history,
    out,
    cell_s, count_s, stage, got_rows, got_ids, onehots, got3, total, chunks, result,
    small_sem, id_send, id_recv, row_send, row_recv, part_send, part_recv, all_send, all_recv,
):
    slab, tile = lax.axis_index("slab"), lax.axis_index("tile")
    barrier = pltpu.get_barrier_semaphore()
    for k in range(1, TILES):
        pl.semaphore_signal(barrier, inc=1, device_id=(slab, (tile + k) % TILES), device_id_type=MESH)
    for k in range(1, SLABS):
        pl.semaphore_signal(barrier, inc=1, device_id=((slab + k) % SLABS, tile), device_id_type=MESH)
    small = [(cell, cell_s), (count, count_s)]
    for i, (src, dst) in enumerate(small):
        pltpu.make_async_copy(src, dst, small_sem.at[i]).start()
    for i, (src, dst) in enumerate(small):
        pltpu.make_async_copy(src, dst, small_sem.at[i]).wait()
    shape = (CAP, LANES)

    def owner_of(k):
        return (((tile >> 2) + k // SIDE) & 3) * SIDE + ((tile + k) & 3)

    def ids_to(k):
        owner = owner_of(k)
        return pltpu.make_async_remote_copy(
            src_ref=ids.at[owner], dst_ref=got_ids.at[k], send_sem=id_send.at[k], recv_sem=id_recv.at[k],
            device_id=(slab, owner), device_id_type=MESH,
        )

    def rows_to(k, h):
        return pltpu.make_async_remote_copy(
            src_ref=stage.at[h, k], dst_ref=got_rows.at[h, k],
            send_sem=row_send.at[h, k], recv_sem=row_recv.at[h, k],
            device_id=(slab, owner_of(k)), device_id_type=MESH,
        )

    def make_rows(k):
        j = owner_of(k)
        base = pl.multiple_of(j * CAP, CAP)
        for i in range(CAP):
            got3[pl.ds(i, 1), :] = lam3[pl.ds(cell_s[base + i] >> 7, 1), :]
        lane = jnp.broadcast_to((cells[pl.ds(j, 1), :] & 127).astype(jnp.float32), shape).T
        here = lane.astype(jnp.int32) == lax.broadcasted_iota(jnp.int32, shape, 1)
        acc = jnp.zeros((CAP, K), jnp.float32)
        for n, got in enumerate((got1[pl.ds(base, CAP), :], got2[pl.ds(base, CAP), :], got3[...])):
            value = jnp.sum(jnp.where(here, got, 0.0), axis=1, keepdims=True)
            acc = acc + value * history[n, pl.ds(base, CAP), :].astype(jnp.float32)
        live = lax.broadcasted_iota(jnp.int32, (CAP, K), 0) < count_s[j]
        acc = jnp.where(live, acc, 0.0).astype(jnp.bfloat16)
        for h in range(HALVES):
            stage[h, k] = acc[:, h * WIDE:(h + 1) * WIDE]

    def onehot_of(named):
        return (
            jnp.broadcast_to(named - tile * OWN, (OWN, CAP)) == lax.broadcasted_iota(jnp.int32, (OWN, CAP), 0)
        ).astype(jnp.bfloat16)

    for k in OFFSETS:
        make_rows(k)
    pl.semaphore_wait(barrier, TILES + SLABS - 2)
    for k in OFFSETS:
        ids_to(k).start()
    for h in range(HALVES):
        for k in OFFSETS:
            rows_to(k, h).start()
    make_rows(0)
    onehots[0] = onehot_of(ids[tile])
    for h in range(HALVES):
        total[h] = jnp.dot(onehots[0], stage[h, 0], preferred_element_type=jnp.float32)
    for k in OFFSETS:
        ids_to(k).wait_recv()
        onehots[k] = onehot_of(got_ids[k])

    mine = pl.ds(pl.multiple_of(slab * PART, PART), PART)

    def to_slab(k, h):
        owner = (slab + k) % SLABS
        return pltpu.make_async_remote_copy(
            src_ref=total.at[h, pl.ds(pl.multiple_of(owner * PART, PART), PART)], dst_ref=chunks.at[h, k],
            send_sem=part_send.at[h, k], recv_sem=part_recv.at[h, k],
            device_id=(owner, tile), device_id_type=MESH,
        )

    def to_all(k, h, back=False):
        owner = (slab + SLABS - k) % SLABS if back else slab
        return pltpu.make_async_remote_copy(
            src_ref=result.at[h, mine],
            dst_ref=result.at[h, pl.ds(pl.multiple_of(owner * PART, PART), PART)],
            send_sem=all_send.at[h, k], recv_sem=all_recv.at[h, k],
            device_id=((slab + k) % SLABS, tile), device_id_type=MESH,
        )

    def add_rows(h, which):
        for k in which:
            rows_to(k, h).wait_recv()
            total[h] += jnp.dot(onehots[k], got_rows[h, k], preferred_element_type=jnp.float32)

    def spread(h):
        for k in range(1, SLABS):
            to_slab(k, h).start()

    def gather(h):
        whole = total[h, mine, :]
        for k in range(1, SLABS):
            to_slab(k, h).wait_recv()
            whole = whole + chunks[h, k]
        result[h, mine, :] = whole
        for k in range(1, SLABS):
            to_all(k, h).start()

    add_rows(0, OFFSETS)
    spread(0)
    add_rows(1, OFFSETS[:10])
    gather(0)
    add_rows(1, OFFSETS[10:])
    spread(1)
    gather(1)
    for h in range(HALVES):
        for k in range(1, SLABS):
            to_all(k, h, True).wait_recv()
        out[:, h * WIDE:(h + 1) * WIDE] = result[h]
    for k in OFFSETS:
        ids_to(k).wait_send()
        for h in range(HALVES):
            rows_to(k, h).wait_send()
    for h in range(HALVES):
        for k in range(1, SLABS):
            to_slab(k, h).wait_send()
            to_all(k, h).wait_send()


SMEM = pl.BlockSpec(memory_space=pltpu.SMEM)
VMEM = pl.BlockSpec(memory_space=pltpu.VMEM)
HBM = pl.BlockSpec(memory_space=pltpu.HBM)
F32, BF16, I32 = jnp.float32, jnp.bfloat16, jnp.int32
DMA = pltpu.SemaphoreType.DMA
FIELD = (CZ, CY, SUB, LANES)


def in_vmem(*arrays):
    return [pltpu.with_memory_space_constraint(array, pltpu.VMEM) for array in arrays]


def in_hbm(*arrays):
    return [pltpu.with_memory_space_constraint(array, pltpu.HBM) for array in arrays]


def on_device(adjoint, adjoint_prev, courant, wall_cell, wall_patch, block_count, wall_damp, history):
    field = pltpu.VMEM(FIELD, F32)
    picked = pltpu.VMEM((SLOTS, LANES), F32)
    cells = wall_cell.reshape(TILES, CAP)
    damps = wall_damp.reshape(TILES, CAP)
    cell_s, count_s = pltpu.SMEM((SLOTS,), I32), pltpu.SMEM((TILES,), I32)
    keep, lam0, before, cour = pl.pallas_call(
        damp_kernel,
        out_shape=(pltpu.VMEM((FLAT, LANES), F32), field, field, field),
        in_specs=[HBM] * 6,
        out_specs=(VMEM,) * 4,
        scratch_shapes=[
            pltpu.SMEM((TILES, CAP), I32), count_s,
            pltpu.VMEM((TILES, CAP), I32), pltpu.VMEM((TILES, CAP), F32), pltpu.VMEM((TILES, CAP), I32),
            picked, pltpu.VMEM((CAP, LANES), F32), DMA((3,)), DMA((4,)),
        ],
        compiler_params=pltpu.CompilerParams(vmem_limit_bytes=4 * MIB),
        name="damp",
    )(*in_hbm(block_count, cells, damps, adjoint, adjoint_prev, courant))
    keep = keep.reshape(FIELD)
    zlayer, ylayer = (2, CY + 2, SUB, LANES), (2, CZ, SUB, LANES)
    lam1, lam2, begun, layer_z, layer_y, got1, begun2 = pl.pallas_call(
        steps_kernel,
        out_shape=(field, field, field, pltpu.VMEM(zlayer, F32), pltpu.VMEM(ylayer, F32), picked, picked),
        in_specs=[VMEM] * 4 + [HBM],
        out_specs=(VMEM,) * 7,
        scratch_shapes=[
            pltpu.VMEM((2, *zlayer), F32), pltpu.VMEM((2, *ylayer), F32), cell_s,
            DMA, DMA((3, 8)), DMA((3, 8)),
        ],
        compiler_params=pltpu.CompilerParams(
            vmem_limit_bytes=5 * MIB, collective_id=0, has_side_effects=True
        ),
        name="steps",
    )(*in_vmem(lam0, before, cour, keep), *in_hbm(wall_cell))
    whole = jax.ShapeDtypeStruct((CZ, CY, NX), F32)
    lam3, final, previous, got2 = pl.pallas_call(
        last_kernel,
        out_shape=(field, whole, whole, picked),
        in_specs=[VMEM] * 8 + [HBM],
        out_specs=(VMEM, HBM, HBM, VMEM),
        scratch_shapes=[cell_s, DMA, DMA((3, SUB))],
        input_output_aliases={2: 0, 3: 3},
        compiler_params=pltpu.CompilerParams(vmem_limit_bytes=4 * MIB),
        name="last",
    )(*in_vmem(lam1, lam2, begun, begun2, layer_z, layer_y, keep, cour), *in_hbm(wall_cell))
    gradient = pl.pallas_call(
        patch_kernel,
        out_shape=jax.ShapeDtypeStruct((OWN, K), F32),
        in_specs=[HBM, HBM] + [VMEM] * 6,
        out_specs=VMEM,
        scratch_shapes=[
            cell_s, count_s,
            pltpu.VMEM((HALVES, TILES, CAP, WIDE), BF16), pltpu.VMEM((HALVES, TILES, CAP, WIDE), BF16),
            pltpu.VMEM((TILES, 1, CAP), I32), pltpu.VMEM((TILES, OWN, CAP), BF16), pltpu.VMEM((CAP, LANES), F32),
            pltpu.VMEM((HALVES, OWN, WIDE), F32), pltpu.VMEM((HALVES, SLABS, PART, WIDE), F32),
            pltpu.VMEM((HALVES, OWN, WIDE), F32),
            DMA((2,)), DMA((TILES,)), DMA((TILES,)), DMA((HALVES, TILES)), DMA((HALVES, TILES)),
            DMA((HALVES, SLABS)), DMA((HALVES, SLABS)), DMA((HALVES, SLABS)), DMA((HALVES, SLABS)),
        ],
        compiler_params=pltpu.CompilerParams(
            vmem_limit_bytes=8 * MIB, collective_id=1, has_side_effects=True
        ),
        name="patch",
    )(
        *in_hbm(wall_cell, block_count),
        wall_patch.reshape(TILES, 1, CAP), cells,
        *in_vmem(lam3.reshape(FLAT, LANES), got1, got2), history,
    )
    return gradient, final, previous


def solution(mesh):
    return jax.shard_map(
        on_device,
        mesh=mesh,
        in_specs=(
            P("slab", "tile", None),
            P("slab", "tile", None),
            P("slab", "tile", None),
            P(("slab", "tile")),
            P(("slab", "tile")),
            P(("slab", "tile")),
            P(("slab", "tile")),
            P(None, ("slab", "tile"), None),
        ),
        out_specs=(P("tile", None), P("slab", "tile", None), P("slab", "tile", None)),
        check_vma=False,
    )
```

```python
import jax
import jax.numpy as jnp
from jax import lax
from jax.experimental import pallas as pl
from jax.experimental.pallas import tpu as pltpu
from jax.sharding import PartitionSpec as P

PATCHES = 4096
CZ, CY, NX, LANES = 16, 64, 1024, 128
SUB = NX // LANES
FLAT = CZ * CY * SUB
SLOTS, K, STEPS = 2048, 256, 3
SLABS, TILES, SIDE = 8, 16, 4
CAP = SLOTS // TILES
OWN = PATCHES // TILES
HALVES, WIDE = 2, 128
PART = OWN // SLABS
MESH = pl.DeviceIdType.MESH
MIB = 1 << 20
NT = (((1,), (1,)), ((), ()))
DIRS = [(-1, 0), (1, 0), (-1, -1), (-1, 1), (1, -1), (1, 1), (0, -1), (0, 1)]
OFFSETS = sorted(
    range(1, TILES),
    key=lambda k: -min(k // SIDE, SIDE - k // SIDE) - min(k % SIDE, SIDE - k % SIDE),
)
PICKS = SLOTS // CZ


def damp_kernel(
    count, cells, damps, adjoint, adjoint_prev, courant,
    keep, lam0, before, cour,
    row_s, count_s, cell_v, damp_v, row_v, inc, old, load_sem, small_sem,
):
    small = [(count, count_s), (cells, cell_v), (damps, damp_v)]
    for i, (src, dst) in enumerate(small):
        pltpu.make_async_copy(src, dst, small_sem.at[i]).start()
    for i, (src, dst) in enumerate(((adjoint, lam0), (adjoint_prev, before), (courant, cour))):
        for s in range(SUB):
            pltpu.make_async_copy(
                src.at[:, :, pl.ds(s * LANES, LANES)], dst.at[:, :, s, :], load_sem.at[i]
            ).start()

    def clear(i, carry):
        keep[pl.ds(pl.multiple_of(i * 128, 128), 128), :] = jnp.ones((128, LANES), jnp.float32)
        return carry

    lax.fori_loop(0, FLAT // 128, clear, 0)
    for i, (src, dst) in enumerate(small):
        pltpu.make_async_copy(src, dst, small_sem.at[i]).wait()
    row_v[...] = cell_v[...] >> 7
    table = pltpu.make_async_copy(row_v, row_s, small_sem.at[3])
    table.start()
    shape = (CAP, LANES)

    def loss(j, carry):
        cell = cell_v[pl.ds(j, 1), :]
        live = lax.broadcasted_iota(jnp.int32, (1, CAP), 1) < count_s[j]
        damp = jnp.where(live, damp_v[pl.ds(j, 1), :], 0.0)
        row = jnp.broadcast_to((cell >> 7).astype(jnp.float32), shape)
        lane = jnp.broadcast_to(cell & 127, shape)
        same = jnp.where(row.T == row, jnp.broadcast_to(damp, shape), 0.0)
        onehot = (lane == lax.broadcasted_iota(jnp.int32, shape, 0)).astype(jnp.bfloat16)
        high = same.astype(jnp.bfloat16)
        rest = same - high.astype(jnp.float32)
        mid = rest.astype(jnp.bfloat16)
        low = (rest - mid.astype(jnp.float32)).astype(jnp.bfloat16)

        def place(part):
            return lax.dot_general(part, onehot, NT, preferred_element_type=jnp.float32)

        inc[pl.ds(pl.multiple_of(j * CAP, CAP), CAP), :] = place(high) + place(mid) + place(low)
        return carry

    lax.fori_loop(0, TILES, loss, 0, unroll=4)
    table.wait()

    def block(j, carry):
        base = pl.multiple_of(j * CAP, CAP)
        for k in range(CAP):
            old[pl.ds(k, 1), :] = keep[pl.ds(row_s[j, k], 1), :]
        old[...] = old[...] - inc[pl.ds(base, CAP), :]
        for k in range(CAP):
            keep[pl.ds(row_s[j, k], 1), :] = old[pl.ds(k, 1), :]
        return carry

    lax.fori_loop(0, TILES, block, 0)
    for i, dst in enumerate((lam0, before, cour)):
        pltpu.make_async_copy(dst, dst, load_sem.at[i]).wait()


def stepper(lam, layer_z, layer_y, before, keep, cour, out, cell_s=None, got=None):
    lane = lax.broadcasted_iota(jnp.int32, (SUB, LANES), 1)
    sub = lax.broadcasted_iota(jnp.int32, (SUB, LANES), 0)
    first_lane, last_lane = lane == 0, lane == LANES - 1
    not_first = jnp.where(sub == 0, 0.0, 1.0)
    not_last = jnp.where(sub == SUB - 1, 0.0, 1.0)
    flat = lam.reshape(FLAT, LANES) if got is not None else None

    def x_sides(q):
        left = pltpu.roll(q, 1, 1)
        right = pltpu.roll(q, LANES - 1, 1)
        left = jnp.where(first_lane, pltpu.roll(left, 1, 0) * not_first, left)
        right = jnp.where(last_lane, pltpu.roll(right, SUB - 1, 0) * not_last, right)
        return left + right

    def cells(z, y):
        if isinstance(z, int) and not 0 <= z < CZ:
            return layer_z[int(z > 0), y + 1]
        if isinstance(y, int) and not 0 <= y < CY:
            return layer_y[int(y > 0), z]
        return lam[z, y]

    def rows(z, first, count, picks=None):
        def parts(y):
            mid = cells(z, y)
            sides = cells(z - 1, y) + cells(z + 1, y)
            quarter = sides * 0.25
            a = mid + quarter
            return mid, sides, a, (a + quarter) * 0.25

        down, here = parts(first - 1), parts(first)
        for k in range(count):
            y = first + k
            up = parts(y + 1)
            mid, sides, a, b = here
            q = a + (down[3] + up[3])
            twice = (sides - 10.0 * mid) + (down[2] + up[2]) + x_sides(q)
            out[z, y] = mid + (mid - before[z, y]) * keep[z, y] + cour[z, y] * (0.5 * twice)
            down, here = here, up
            if got is not None and picks is not None:
                for slot in range(PICKS * k // count, PICKS * (k + 1) // count):
                    at = picks * PICKS + slot
                    got[pl.ds(at, 1), :] = flat[pl.ds(cell_s[at] >> 7, 1), :]

    def inside(first, last):
        def layer(z, carry):
            rows(z, 1, CY - 2, z)
            return carry

        lax.fori_loop(first, last + 1, layer, 0)

    def layers():
        for z in (0, CZ - 1):
            rows(z, 0, CY, z)

    def edges():
        def edge(i, carry):
            for k in range(7):
                rows(1 + 7 * i + k, 0, 1)
                rows(1 + 7 * i + k, CY - 1, 1)
            return carry

        lax.fori_loop(0, (CZ - 2) // 7, edge, 0)

    return inside, layers, edges


def wave_kernel(
    lam0, before, cour, keep, cell, count, cells, ids, history,
    lam2, lam3, out,
    lam1, layer_z, layer_y, sent_z, sent_y, came_z, came_y, got1, got2, got3, cell_s, count_s, cell_v, id_v, hist,
    stage, got_rows, got_ids, onehots, total, chunks, result,
    load_sem, send_sem, recv_sem, id_send, id_recv, row_send, row_recv, part_send, part_recv, all_send, all_recv,
):
    slab, tile = lax.axis_index("slab"), lax.axis_index("tile")

    def has(dz, dy):
        z, y = slab + dz, tile + dy
        return (z >= 0) & (z < SLABS) & (y >= 0) & (y < TILES)

    barrier = pltpu.get_barrier_semaphore()
    for dz, dy in DIRS[2:6]:
        @pl.when(has(dz, dy))
        def _():
            pl.semaphore_signal(barrier, inc=1, device_id=(slab + dz, tile + dy), device_id_type=MESH)
    for k in range(1, SLABS):
        pl.semaphore_signal(barrier, inc=1, device_id=((slab + k) % SLABS, tile), device_id_type=MESH)
    for k in range(1, TILES):
        pl.semaphore_signal(barrier, inc=1, device_id=(slab, (tile + k) % TILES), device_id_type=MESH)
    zs = jnp.where((slab == 0) | (slab == SLABS - 1), 1, 2)
    ys = jnp.where((tile == 0) | (tile == TILES - 1), 1, 2)
    loads = [(cell, cell_s), (count, count_s), (cells, cell_v), (ids, id_v), (history, hist)]
    loads = [pltpu.make_async_copy(src, dst, load_sem.at[i]) for i, (src, dst) in enumerate(loads)]
    for load in loads:
        load.start()
    lams = (lam0, lam1, lam2)
    zlayers = [layer_z.at[n] for n in range(STEPS)]
    ylayers = [layer_y.at[n] for n in range(STEPS)]

    for n in range(STEPS):
        for side, no_z, no_y in ((0, slab == 0, tile == 0), (1, slab == SLABS - 1, tile == TILES - 1)):
            @pl.when(no_z)
            def _():
                zlayers[n][side] = jnp.zeros((CY + 2, SUB, LANES), jnp.float32)
            @pl.when(no_y)
            def _():
                ylayers[n][side] = jnp.zeros((CZ, SUB, LANES), jnp.float32)
                for z in range(2):
                    zlayers[n][z, side * (CY + 1)] = jnp.zeros((SUB, LANES), jnp.float32)

    def pack_z(n):
        for side in range(2):
            sent_z[n, side] = lams[n][side * (CZ - 1)].reshape(CY // 2, 2 * SUB, LANES).astype(jnp.bfloat16)

    def pack_y(n):
        for side in range(2):
            sent_y[n, side] = lams[n][:, side * (CY - 1)].reshape(CZ // 2, 2 * SUB, LANES).astype(jnp.bfloat16)

    def message(n, d):
        dz, dy = DIRS[d]
        if dy == 0:
            src, dst = sent_z.at[n, int(dz > 0)], came_z.at[n, int(dz < 0)]
        elif dz == 0:
            src, dst = sent_y.at[n, int(dy > 0)], came_y.at[n, int(dy < 0)]
        else:
            src = lams[n].at[0 if dz < 0 else CZ - 1, 0 if dy < 0 else CY - 1]
            dst = zlayers[n].at[int(dz < 0), CY + 1 if dy < 0 else 0]
        return pltpu.make_async_remote_copy(
            src_ref=src,
            dst_ref=dst,
            send_sem=send_sem.at[n, d],
            recv_sem=recv_sem.at[n, d],
            device_id=(slab + dz, tile + dy),
            device_id_type=MESH,
        )

    def send(n, which):
        for d in which:
            @pl.when(has(*DIRS[d]))
            def _():
                message(n, d).start()

    def receive(n):
        for d in range(8):
            dz, dy = DIRS[d]
            @pl.when(has(-dz, -dy))
            def _():
                message(n, d).wait_recv()
                if dy == 0:
                    side = int(dz < 0)
                    zlayers[n][side, pl.ds(1, CY)] = (
                        came_z[n, side].astype(jnp.float32).reshape(CY, SUB, LANES)
                    )
                elif dz == 0:
                    side = int(dy < 0)
                    ylayers[n][side] = came_y[n, side].astype(jnp.float32).reshape(CZ, SUB, LANES)

    def owner_of(k):
        return (((tile >> 2) + k // SIDE) & 3) * SIDE + ((tile + k) & 3)

    def ids_to(k):
        owner = owner_of(k)
        return pltpu.make_async_remote_copy(
            src_ref=id_v.at[owner], dst_ref=got_ids.at[k], send_sem=id_send.at[k], recv_sem=id_recv.at[k],
            device_id=(slab, owner), device_id_type=MESH,
        )

    first = stepper(lam0, zlayers[0], ylayers[0], before, keep, cour, lam1)
    second = stepper(lam1, zlayers[1], ylayers[1], lam0, keep, cour, lam2, cell_s, got1)
    third = stepper(lam2, zlayers[2], ylayers[2], lam1, keep, cour, lam3, cell_s, got2)

    def outer(n, step):
        receive(n - 1)
        step[1]()
        pack_z(n)
        send(n, range(6))
        step[2]()
        pack_y(n)
        send(n, range(6, 8))

    pack_z(0)
    pack_y(0)
    first[0](1, 5)
    pl.semaphore_wait(barrier, zs * ys + SLABS + TILES - 2)
    send(0, range(8))
    first[0](6, CZ - 2)
    outer(1, first)
    for load in loads:
        load.wait()
    second[0](1, CZ - 2)
    for k in OFFSETS:
        ids_to(k).start()
    outer(2, second)
    third[0](1, CZ - 2)
    receive(2)
    third[1]()
    third[2]()
    flat3 = lam3.reshape(FLAT, LANES)
    shape = (CAP, LANES)

    def rows_to(k, h):
        return pltpu.make_async_remote_copy(
            src_ref=stage.at[h, k], dst_ref=got_rows.at[h, k],
            send_sem=row_send.at[h, k], recv_sem=row_recv.at[h, k],
            device_id=(slab, owner_of(k)), device_id_type=MESH,
        )

    def make_rows(k):
        j = owner_of(k)
        base = pl.multiple_of(j * CAP, CAP)
        for i in range(CAP):
            got3[pl.ds(i, 1), :] = flat3[pl.ds(cell_s[base + i] >> 7, 1), :]
        lane = jnp.broadcast_to((cell_v[pl.ds(j, 1), :] & 127).astype(jnp.float32), shape).T
        here = lane.astype(jnp.int32) == lax.broadcasted_iota(jnp.int32, shape, 1)
        acc = jnp.zeros((CAP, K), jnp.float32)
        for n, got in enumerate((got1[pl.ds(base, CAP), :], got2[pl.ds(base, CAP), :], got3[...])):
            value = jnp.sum(jnp.where(here, got, 0.0), axis=1, keepdims=True)
            acc = acc + value * hist[n, pl.ds(base, CAP), :].astype(jnp.float32)
        live = lax.broadcasted_iota(jnp.int32, (CAP, K), 0) < count_s[j]
        acc = jnp.where(live, acc, 0.0).astype(jnp.bfloat16)
        for h in range(HALVES):
            stage[h, k] = acc[:, h * WIDE:(h + 1) * WIDE]

    def onehot_of(named):
        return (
            jnp.broadcast_to(named - tile * OWN, (OWN, CAP)) == lax.broadcasted_iota(jnp.int32, (OWN, CAP), 0)
        ).astype(jnp.bfloat16)

    for k in OFFSETS:
        make_rows(k)
        rows_to(k, 0).start()
    for k in OFFSETS:
        rows_to(k, 1).start()
    make_rows(0)
    onehots[0] = onehot_of(id_v[tile])
    for h in range(HALVES):
        total[h] = jnp.dot(onehots[0], stage[h, 0], preferred_element_type=jnp.float32)
    for k in OFFSETS:
        ids_to(k).wait_recv()
        onehots[k] = onehot_of(got_ids[k])

    mine = pl.ds(pl.multiple_of(slab * PART, PART), PART)

    def to_slab(k, h):
        owner = (slab + k) % SLABS
        return pltpu.make_async_remote_copy(
            src_ref=total.at[h, pl.ds(pl.multiple_of(owner * PART, PART), PART)], dst_ref=chunks.at[h, k],
            send_sem=part_send.at[h, k], recv_sem=part_recv.at[h, k],
            device_id=(owner, tile), device_id_type=MESH,
        )

    def to_all(k, h, back=False):
        owner = (slab + SLABS - k) % SLABS if back else slab
        return pltpu.make_async_remote_copy(
            src_ref=result.at[h, mine],
            dst_ref=result.at[h, pl.ds(pl.multiple_of(owner * PART, PART), PART)],
            send_sem=all_send.at[h, k], recv_sem=all_recv.at[h, k],
            device_id=((slab + k) % SLABS, tile), device_id_type=MESH,
        )

    def add_rows(h, which):
        for k in which:
            rows_to(k, h).wait_recv()
            total[h] += jnp.dot(onehots[k], got_rows[h, k], preferred_element_type=jnp.float32)

    def spread(h):
        for k in range(1, SLABS):
            to_slab(k, h).start()

    def gather(h):
        whole = total[h, mine, :]
        for k in range(1, SLABS):
            to_slab(k, h).wait_recv()
            whole = whole + chunks[h, k]
        result[h, mine, :] = whole.astype(jnp.bfloat16)
        for k in range(1, SLABS):
            to_all(k, h).start()

    add_rows(0, OFFSETS)
    spread(0)
    add_rows(1, OFFSETS[:10])
    gather(0)
    add_rows(1, OFFSETS[10:])
    spread(1)
    gather(1)
    for h in range(HALVES):
        for k in range(1, SLABS):
            to_all(k, h, True).wait_recv()
        out[:, h * WIDE:(h + 1) * WIDE] = result[h].astype(jnp.float32)
    for n in range(STEPS):
        for d in range(8):
            @pl.when(has(*DIRS[d]))
            def _():
                message(n, d).wait_send()
    for k in OFFSETS:
        ids_to(k).wait_send()
        for h in range(HALVES):
            rows_to(k, h).wait_send()
    for h in range(HALVES):
        for k in range(1, SLABS):
            to_slab(k, h).wait_send()
            to_all(k, h).wait_send()


def write_kernel(lam2, lam3, result, gradient, final, previous, out_sem, sum_sem):
    copies = [pltpu.make_async_copy(result, gradient, sum_sem)]
    for i, (src, dst) in enumerate(((lam2, previous), (lam3, final))):
        for s in range(SUB):
            copies.append(
                pltpu.make_async_copy(src.at[:, :, s, :], dst.at[:, :, pl.ds(s * LANES, LANES)], out_sem.at[i, s])
            )
    for copy in copies:
        copy.start()
    for copy in copies:
        copy.wait()


VMEM = pl.BlockSpec(memory_space=pltpu.VMEM)
HBM = pl.BlockSpec(memory_space=pltpu.HBM)
F32, BF16, I32 = jnp.float32, jnp.bfloat16, jnp.int32
DMA = pltpu.SemaphoreType.DMA
FIELD = (CZ, CY, SUB, LANES)


def in_vmem(*arrays):
    return [pltpu.with_memory_space_constraint(array, pltpu.VMEM) for array in arrays]


def in_hbm(*arrays):
    return [pltpu.with_memory_space_constraint(array, pltpu.HBM) for array in arrays]


def on_device(adjoint, adjoint_prev, courant, wall_cell, wall_patch, block_count, wall_damp, history):
    field = pltpu.VMEM(FIELD, F32)
    picked = pltpu.VMEM((SLOTS, LANES), F32)
    cells = wall_cell.reshape(TILES, CAP)
    damps = wall_damp.reshape(TILES, CAP)
    count_s = pltpu.SMEM((TILES,), I32)
    keep, lam0, before, cour = pl.pallas_call(
        damp_kernel,
        out_shape=(pltpu.VMEM((FLAT, LANES), F32), field, field, field),
        in_specs=[HBM] * 6,
        out_specs=(VMEM,) * 4,
        scratch_shapes=[
            pltpu.SMEM((TILES, CAP), I32), count_s,
            pltpu.VMEM((TILES, CAP), I32), pltpu.VMEM((TILES, CAP), F32), pltpu.VMEM((TILES, CAP), I32),
            picked, pltpu.VMEM((CAP, LANES), F32), DMA((3,)), DMA((4,)),
        ],
        compiler_params=pltpu.CompilerParams(vmem_limit_bytes=4 * MIB),
        name="damp",
    )(*in_hbm(block_count, cells, damps, adjoint, adjoint_prev, courant))
    keep = keep.reshape(FIELD)
    face_z = pltpu.VMEM((STEPS, 2, CY // 2, 2 * SUB, LANES), BF16)
    face_y = pltpu.VMEM((STEPS, 2, CZ // 2, 2 * SUB, LANES), BF16)
    lam2, lam3, result = pl.pallas_call(
        wave_kernel,
        out_shape=(field, field, pltpu.VMEM((OWN, K), F32)),
        in_specs=[VMEM] * 4 + [HBM] * 5,
        out_specs=(VMEM,) * 3,
        scratch_shapes=[
            field, pltpu.VMEM((STEPS, 2, CY + 2, SUB, LANES), F32), pltpu.VMEM((STEPS, 2, CZ, SUB, LANES), F32),
            face_z, face_y, face_z, face_y,
            picked, picked, pltpu.VMEM((CAP, LANES), F32),
            pltpu.SMEM((SLOTS,), I32), count_s, pltpu.VMEM((TILES, CAP), I32), pltpu.VMEM((TILES, 1, CAP), I32),
            pltpu.VMEM((STEPS, SLOTS, K), BF16),
            pltpu.VMEM((HALVES, TILES, CAP, WIDE), BF16), pltpu.VMEM((HALVES, TILES, CAP, WIDE), BF16),
            pltpu.VMEM((TILES, 1, CAP), I32), pltpu.VMEM((TILES, OWN, CAP), BF16),
            pltpu.VMEM((HALVES, OWN, WIDE), F32), pltpu.VMEM((HALVES, SLABS, PART, WIDE), F32),
            pltpu.VMEM((HALVES, OWN, WIDE), BF16),
            DMA((5,)), DMA((STEPS, 8)), DMA((STEPS, 8)),
            DMA((TILES,)), DMA((TILES,)), DMA((HALVES, TILES)), DMA((HALVES, TILES)),
            DMA((HALVES, SLABS)), DMA((HALVES, SLABS)), DMA((HALVES, SLABS)), DMA((HALVES, SLABS)),
        ],
        compiler_params=pltpu.CompilerParams(
            vmem_limit_bytes=20 * MIB, collective_id=0, has_side_effects=True
        ),
        name="wave",
    )(
        *in_vmem(lam0, before, cour, keep),
        *in_hbm(wall_cell, block_count, cells, wall_patch.reshape(TILES, 1, CAP), history),
    )
    whole = jax.ShapeDtypeStruct((CZ, CY, NX), F32)
    gradient, final, previous = pl.pallas_call(
        write_kernel,
        out_shape=(jax.ShapeDtypeStruct((OWN, K), F32), whole, whole),
        in_specs=[VMEM] * 3,
        out_specs=(HBM,) * 3,
        scratch_shapes=[DMA((2, SUB)), DMA],
        compiler_params=pltpu.CompilerParams(vmem_limit_bytes=MIB),
        name="write",
    )(*in_vmem(lam2, lam3, result))
    return gradient, final, previous


def solution(mesh):
    return jax.shard_map(
        on_device,
        mesh=mesh,
        in_specs=(
            P("slab", "tile", None),
            P("slab", "tile", None),
            P("slab", "tile", None),
            P(("slab", "tile")),
            P(("slab", "tile")),
            P(("slab", "tile")),
            P(("slab", "tile")),
            P(None, ("slab", "tile"), None),
        ),
        out_specs=(P("tile", None), P("slab", "tile", None), P("slab", "tile", None)),
        check_vma=False,
    )
```

```python
import jax
import jax.numpy as jnp
from jax import lax
from jax.experimental import pallas as pl
from jax.experimental.pallas import tpu as pltpu
from jax.sharding import PartitionSpec as P

PATCHES = 4096
CZ, CY, NX, LANES = 16, 64, 1024, 128
SUB = NX // LANES
FLAT = CZ * CY * SUB
SLOTS, K, STEPS = 2048, 256, 3
SLABS, TILES, SIDE = 8, 16, 4
CAP = SLOTS // TILES
OWN = PATCHES // TILES
HALVES, WIDE = 2, 128
FAR_SLABS = (4, 3, 5, 2, 6, 1, 7)
PART = OWN // SLABS
MESH = pl.DeviceIdType.MESH
MIB = 1 << 20
NT = (((1,), (1,)), ((), ()))
DIRS = [(-1, 0), (1, 0), (-1, -1), (-1, 1), (1, -1), (1, 1), (0, -1), (0, 1)]
OFFSETS = sorted(
    range(1, TILES),
    key=lambda k: -min(k // SIDE, SIDE - k // SIDE) - min(k % SIDE, SIDE - k % SIDE),
)
PICKS = SLOTS // CZ


def damp_kernel(
    count, cells, damps, adjoint, adjoint_prev, courant,
    keep, lam0, before, cour,
    row_s, count_s, cell_v, damp_v, row_v, inc, old, load_sem, small_sem,
):
    small = [(count, count_s), (cells, cell_v), (damps, damp_v)]
    for i, (src, dst) in enumerate(small):
        pltpu.make_async_copy(src, dst, small_sem.at[i]).start()
    for i, (src, dst) in enumerate(((adjoint, lam0), (adjoint_prev, before), (courant, cour))):
        for s in range(SUB):
            pltpu.make_async_copy(
                src.at[:, :, pl.ds(s * LANES, LANES)], dst.at[:, :, s, :], load_sem.at[i]
            ).start()

    def clear(i, carry):
        keep[pl.ds(pl.multiple_of(i * 128, 128), 128), :] = jnp.ones((128, LANES), jnp.float32)
        return carry

    lax.fori_loop(0, FLAT // 128, clear, 0)
    for i, (src, dst) in enumerate(small):
        pltpu.make_async_copy(src, dst, small_sem.at[i]).wait()
    row_v[...] = cell_v[...] >> 7
    table = pltpu.make_async_copy(row_v, row_s, small_sem.at[3])
    table.start()
    shape = (CAP, LANES)

    def loss(j, carry):
        cell = cell_v[pl.ds(j, 1), :]
        live = lax.broadcasted_iota(jnp.int32, (1, CAP), 1) < count_s[j]
        damp = jnp.where(live, damp_v[pl.ds(j, 1), :], 0.0)
        row = jnp.broadcast_to((cell >> 7).astype(jnp.float32), shape)
        lane = jnp.broadcast_to(cell & 127, shape)
        same = jnp.where(row.T == row, jnp.broadcast_to(damp, shape), 0.0)
        onehot = (lane == lax.broadcasted_iota(jnp.int32, shape, 0)).astype(jnp.bfloat16)
        high = same.astype(jnp.bfloat16)
        rest = same - high.astype(jnp.float32)
        mid = rest.astype(jnp.bfloat16)
        low = (rest - mid.astype(jnp.float32)).astype(jnp.bfloat16)

        def place(part):
            return lax.dot_general(part, onehot, NT, preferred_element_type=jnp.float32)

        inc[pl.ds(pl.multiple_of(j * CAP, CAP), CAP), :] = place(high) + place(mid) + place(low)
        return carry

    lax.fori_loop(0, TILES, loss, 0, unroll=8)
    table.wait()

    def block(j, carry):
        base = pl.multiple_of(j * CAP, CAP)
        for k in range(CAP):
            old[pl.ds(k, 1), :] = keep[pl.ds(row_s[j, k], 1), :]
        old[...] = old[...] - inc[pl.ds(base, CAP), :]
        for k in range(CAP):
            keep[pl.ds(row_s[j, k], 1), :] = old[pl.ds(k, 1), :]
        return carry

    lax.fori_loop(0, TILES, block, 0)
    for i, dst in enumerate((lam0, before, cour)):
        pltpu.make_async_copy(dst, dst, load_sem.at[i]).wait()


def stepper(lam, layer_z, layer_y, before, keep, cour, out, cell_s=None, got=None):
    lane = lax.broadcasted_iota(jnp.int32, (SUB, LANES), 1)
    sub = lax.broadcasted_iota(jnp.int32, (SUB, LANES), 0)
    first_lane, last_lane = lane == 0, lane == LANES - 1
    not_first = jnp.where(sub == 0, 0.0, 1.0)
    not_last = jnp.where(sub == SUB - 1, 0.0, 1.0)
    flat = lam.reshape(FLAT, LANES) if got is not None else None

    def x_sides(q):
        left = pltpu.roll(q, 1, 1)
        right = pltpu.roll(q, LANES - 1, 1)
        left = jnp.where(first_lane, pltpu.roll(left, 1, 0) * not_first, left)
        right = jnp.where(last_lane, pltpu.roll(right, SUB - 1, 0) * not_last, right)
        return left + right

    def cells(z, y):
        if isinstance(z, int) and not 0 <= z < CZ:
            return layer_z[int(z > 0), y + 1]
        if isinstance(y, int) and not 0 <= y < CY:
            return layer_y[int(y > 0), z]
        return lam[z, y]

    def rows(z, first, count, picks=None):
        def parts(y):
            mid = cells(z, y)
            sides = cells(z - 1, y) + cells(z + 1, y)
            quarter = sides * 0.25
            a = mid + quarter
            return mid, sides, a, (a + quarter) * 0.25

        down, here = parts(first - 1), parts(first)
        for k in range(count):
            y = first + k
            up = parts(y + 1)
            mid, sides, a, b = here
            q = a + (down[3] + up[3])
            twice = (sides - 10.0 * mid) + (down[2] + up[2]) + x_sides(q)
            out[z, y] = mid + (mid - before[z, y]) * keep[z, y] + cour[z, y] * (0.5 * twice)
            down, here = here, up
            if got is not None and picks is not None:
                for slot in range(PICKS * k // count, PICKS * (k + 1) // count):
                    at = picks * PICKS + slot
                    got[pl.ds(at, 1), :] = flat[pl.ds(cell_s[at] >> 7, 1), :]

    def inside(first, last):
        def layer(z, carry):
            rows(z, 1, CY - 2, z)
            return carry

        lax.fori_loop(first, last + 1, layer, 0)

    def layers():
        for z in (0, CZ - 1):
            rows(z, 1, CY - 2, z)

    def edges():
        def edge(i, carry):
            for k in range(7):
                rows(1 + 7 * i + k, 0, 1)
                rows(1 + 7 * i + k, CY - 1, 1)
            return carry

        lax.fori_loop(0, (CZ - 2) // 7, edge, 0)
        for z in (0, CZ - 1):
            rows(z, 0, 1)
            rows(z, CY - 1, 1)

    return inside, layers, edges


def wave_kernel(
    lam0, before, cour, keep, cell, count, cells, ids, history,
    lam2, lam3, out,
    lam1, layer_z, layer_y, sent_z, sent_y, came_z, came_y, got1, got2, got3, cell_s, count_s, cell_v, id_v, hist,
    stage, got_rows, got_ids, onehots, total, chunks, result,
    load_sem, send_sem, recv_sem, id_send, id_recv, row_send, row_recv, part_send, part_recv, all_send, all_recv,
):
    slab, tile = lax.axis_index("slab"), lax.axis_index("tile")

    def has(dz, dy):
        z, y = slab + dz, tile + dy
        return (z >= 0) & (z < SLABS) & (y >= 0) & (y < TILES)

    barrier = pltpu.get_barrier_semaphore()
    for dz, dy in DIRS[2:6]:
        @pl.when(has(dz, dy))
        def _():
            pl.semaphore_signal(barrier, inc=1, device_id=(slab + dz, tile + dy), device_id_type=MESH)
    for k in range(1, SLABS):
        pl.semaphore_signal(barrier, inc=1, device_id=((slab + k) % SLABS, tile), device_id_type=MESH)
    for k in range(1, TILES):
        pl.semaphore_signal(barrier, inc=1, device_id=(slab, (tile + k) % TILES), device_id_type=MESH)
    zs = jnp.where((slab == 0) | (slab == SLABS - 1), 1, 2)
    ys = jnp.where((tile == 0) | (tile == TILES - 1), 1, 2)
    loads = [(cell, cell_s), (count, count_s), (cells, cell_v), (ids, id_v), (history, hist)]
    loads = [pltpu.make_async_copy(src, dst, load_sem.at[i]) for i, (src, dst) in enumerate(loads)]
    for load in loads:
        load.start()
    lams = (lam0, lam1, lam2)
    zlayers = [layer_z.at[n] for n in range(STEPS)]
    ylayers = [layer_y.at[n] for n in range(STEPS)]

    for n in range(STEPS):
        for side, no_z, no_y in ((0, slab == 0, tile == 0), (1, slab == SLABS - 1, tile == TILES - 1)):
            @pl.when(no_z)
            def _():
                zlayers[n][side] = jnp.zeros((CY + 2, SUB, LANES), jnp.float32)
            @pl.when(no_y)
            def _():
                ylayers[n][side] = jnp.zeros((CZ, SUB, LANES), jnp.float32)
                for z in range(2):
                    zlayers[n][z, side * (CY + 1)] = jnp.zeros((SUB, LANES), jnp.float32)

    def pack_z(n):
        for side in range(2):
            sent_z[n, side] = lams[n][side * (CZ - 1)].reshape(CY // 2, 2 * SUB, LANES).astype(jnp.bfloat16)

    def pack_y(n):
        for side in range(2):
            sent_y[n, side] = lams[n][:, side * (CY - 1)].reshape(CZ // 2, 2 * SUB, LANES).astype(jnp.bfloat16)

    def message(n, d):
        dz, dy = DIRS[d]
        if dy == 0:
            src, dst = sent_z.at[n, int(dz > 0)], came_z.at[n, int(dz < 0)]
        elif dz == 0:
            src, dst = sent_y.at[n, int(dy > 0)], came_y.at[n, int(dy < 0)]
        else:
            src = lams[n].at[0 if dz < 0 else CZ - 1, 0 if dy < 0 else CY - 1]
            dst = zlayers[n].at[int(dz < 0), CY + 1 if dy < 0 else 0]
        return pltpu.make_async_remote_copy(
            src_ref=src,
            dst_ref=dst,
            send_sem=send_sem.at[n, d],
            recv_sem=recv_sem.at[n, d],
            device_id=(slab + dz, tile + dy),
            device_id_type=MESH,
        )

    def send(n, which):
        for d in which:
            @pl.when(has(*DIRS[d]))
            def _():
                message(n, d).start()

    def receive(n):
        for d in range(8):
            dz, dy = DIRS[d]
            @pl.when(has(-dz, -dy))
            def _():
                message(n, d).wait_recv()
                if dy == 0:
                    side = int(dz < 0)
                    zlayers[n][side, pl.ds(1, CY)] = (
                        came_z[n, side].astype(jnp.float32).reshape(CY, SUB, LANES)
                    )
                elif dz == 0:
                    side = int(dy < 0)
                    ylayers[n][side] = came_y[n, side].astype(jnp.float32).reshape(CZ, SUB, LANES)

    def owner_of(k):
        return (((tile >> 2) + k // SIDE) & 3) * SIDE + ((tile + k) & 3)

    def ids_to(k):
        owner = owner_of(k)
        return pltpu.make_async_remote_copy(
            src_ref=id_v.at[owner], dst_ref=got_ids.at[k], send_sem=id_send.at[k], recv_sem=id_recv.at[k],
            device_id=(slab, owner), device_id_type=MESH,
        )

    first = stepper(lam0, zlayers[0], ylayers[0], before, keep, cour, lam1)
    second = stepper(lam1, zlayers[1], ylayers[1], lam0, keep, cour, lam2, cell_s, got1)
    third = stepper(lam2, zlayers[2], ylayers[2], lam1, keep, cour, lam3, cell_s, got2)

    def outer(n, step):
        receive(n - 1)
        step[2]()
        pack_y(n)
        send(n, range(2, 8))
        step[1]()
        pack_z(n)
        send(n, range(2))

    pack_z(0)
    pack_y(0)
    first[0](1, 5)
    pl.semaphore_wait(barrier, zs * ys + SLABS + TILES - 2)
    send(0, range(8))
    first[0](6, CZ - 2)
    outer(1, first)
    for load in loads:
        load.wait()
    second[0](1, CZ - 2)
    for k in OFFSETS:
        ids_to(k).start()
    outer(2, second)
    third[0](1, CZ - 2)
    receive(2)
    third[1]()
    third[2]()
    flat3 = lam3.reshape(FLAT, LANES)
    shape = (CAP, LANES)

    def rows_to(k, h):
        return pltpu.make_async_remote_copy(
            src_ref=stage.at[h, k], dst_ref=got_rows.at[h, k],
            send_sem=row_send.at[h, k], recv_sem=row_recv.at[h, k],
            device_id=(slab, owner_of(k)), device_id_type=MESH,
        )

    def make_rows(k):
        j = owner_of(k)
        base = pl.multiple_of(j * CAP, CAP)
        for i in range(CAP):
            got3[pl.ds(i, 1), :] = flat3[pl.ds(cell_s[base + i] >> 7, 1), :]
        lane = jnp.broadcast_to((cell_v[pl.ds(j, 1), :] & 127).astype(jnp.float32), shape).T
        here = lane.astype(jnp.int32) == lax.broadcasted_iota(jnp.int32, shape, 1)
        acc = jnp.zeros((CAP, K), jnp.float32)
        for n, got in enumerate((got1[pl.ds(base, CAP), :], got2[pl.ds(base, CAP), :], got3[...])):
            value = jnp.sum(jnp.where(here, got, 0.0), axis=1, keepdims=True)
            acc = acc + value * hist[n, pl.ds(base, CAP), :].astype(jnp.float32)
        live = lax.broadcasted_iota(jnp.int32, (CAP, K), 0) < count_s[j]
        acc = jnp.where(live, acc, 0.0).astype(jnp.bfloat16)
        for h in range(HALVES):
            stage[h, k] = acc[:, h * WIDE:(h + 1) * WIDE]

    def onehot_of(named):
        return (
            jnp.broadcast_to(named - tile * OWN, (OWN, CAP)) == lax.broadcasted_iota(jnp.int32, (OWN, CAP), 0)
        ).astype(jnp.bfloat16)

    for k in OFFSETS:
        make_rows(k)
        rows_to(k, 0).start()
    for k in OFFSETS:
        rows_to(k, 1).start()
    make_rows(0)
    onehots[0] = onehot_of(id_v[tile])
    for h in range(HALVES):
        total[h] = jnp.dot(onehots[0], stage[h, 0], preferred_element_type=jnp.float32)
    for k in OFFSETS:
        ids_to(k).wait_recv()
        onehots[k] = onehot_of(got_ids[k])

    mine = pl.ds(pl.multiple_of(slab * PART, PART), PART)

    def to_slab(k, h):
        owner = (slab + k) % SLABS
        return pltpu.make_async_remote_copy(
            src_ref=total.at[h, pl.ds(pl.multiple_of(owner * PART, PART), PART)], dst_ref=chunks.at[h, k],
            send_sem=part_send.at[h, k], recv_sem=part_recv.at[h, k],
            device_id=(owner, tile), device_id_type=MESH,
        )

    def to_all(k, h, back=False):
        owner = (slab + SLABS - k) % SLABS if back else slab
        return pltpu.make_async_remote_copy(
            src_ref=result.at[h, mine],
            dst_ref=result.at[h, pl.ds(pl.multiple_of(owner * PART, PART), PART)],
            send_sem=all_send.at[h, k], recv_sem=all_recv.at[h, k],
            device_id=((slab + k) % SLABS, tile), device_id_type=MESH,
        )

    def add_rows(h, which):
        for k in which:
            rows_to(k, h).wait_recv()
            total[h] += jnp.dot(onehots[k], got_rows[h, k], preferred_element_type=jnp.float32)

    def spread(h):
        for k in FAR_SLABS:
            to_slab(k, h).start()

    def gather(h):
        whole = total[h, mine, :]
        for k in range(1, SLABS):
            to_slab(k, h).wait_recv()
            whole = whole + chunks[h, k]
        result[h, mine, :] = whole.astype(jnp.bfloat16)
        for k in FAR_SLABS:
            to_all(k, h).start()

    add_rows(0, OFFSETS)
    spread(0)
    add_rows(1, OFFSETS[:10])
    gather(0)
    add_rows(1, OFFSETS[10:])
    spread(1)
    gather(1)
    for h in range(HALVES):
        for k in range(1, SLABS):
            to_all(k, h, True).wait_recv()
        out[:, h * WIDE:(h + 1) * WIDE] = result[h].astype(jnp.float32)
    for n in range(STEPS):
        for d in range(8):
            @pl.when(has(*DIRS[d]))
            def _():
                message(n, d).wait_send()
    for k in OFFSETS:
        ids_to(k).wait_send()
        for h in range(HALVES):
            rows_to(k, h).wait_send()
    for h in range(HALVES):
        for k in range(1, SLABS):
            to_slab(k, h).wait_send()
            to_all(k, h).wait_send()


def write_kernel(lam2, lam3, result, gradient, final, previous, out_sem, sum_sem):
    copies = [pltpu.make_async_copy(result, gradient, sum_sem)]
    for i, (src, dst) in enumerate(((lam2, previous), (lam3, final))):
        for s in range(SUB):
            copies.append(
                pltpu.make_async_copy(src.at[:, :, s, :], dst.at[:, :, pl.ds(s * LANES, LANES)], out_sem.at[i, s])
            )
    for copy in copies:
        copy.start()
    for copy in copies:
        copy.wait()


VMEM = pl.BlockSpec(memory_space=pltpu.VMEM)
HBM = pl.BlockSpec(memory_space=pltpu.HBM)
F32, BF16, I32 = jnp.float32, jnp.bfloat16, jnp.int32
DMA = pltpu.SemaphoreType.DMA
FIELD = (CZ, CY, SUB, LANES)


def in_vmem(*arrays):
    return [pltpu.with_memory_space_constraint(array, pltpu.VMEM) for array in arrays]


def in_hbm(*arrays):
    return [pltpu.with_memory_space_constraint(array, pltpu.HBM) for array in arrays]


def on_device(adjoint, adjoint_prev, courant, wall_cell, wall_patch, block_count, wall_damp, history):
    field = pltpu.VMEM(FIELD, F32)
    picked = pltpu.VMEM((SLOTS, LANES), F32)
    cells = wall_cell.reshape(TILES, CAP)
    damps = wall_damp.reshape(TILES, CAP)
    count_s = pltpu.SMEM((TILES,), I32)
    keep, lam0, before, cour = pl.pallas_call(
        damp_kernel,
        out_shape=(pltpu.VMEM((FLAT, LANES), F32), field, field, field),
        in_specs=[HBM] * 6,
        out_specs=(VMEM,) * 4,
        scratch_shapes=[
            pltpu.SMEM((TILES, CAP), I32), count_s,
            pltpu.VMEM((TILES, CAP), I32), pltpu.VMEM((TILES, CAP), F32), pltpu.VMEM((TILES, CAP), I32),
            picked, pltpu.VMEM((CAP, LANES), F32), DMA((3,)), DMA((4,)),
        ],
        compiler_params=pltpu.CompilerParams(vmem_limit_bytes=4 * MIB),
        name="damp",
    )(*in_hbm(block_count, cells, damps, adjoint, adjoint_prev, courant))
    keep = keep.reshape(FIELD)
    face_z = pltpu.VMEM((STEPS, 2, CY // 2, 2 * SUB, LANES), BF16)
    face_y = pltpu.VMEM((STEPS, 2, CZ // 2, 2 * SUB, LANES), BF16)
    lam2, lam3, result = pl.pallas_call(
        wave_kernel,
        out_shape=(field, field, pltpu.VMEM((OWN, K), F32)),
        in_specs=[VMEM] * 4 + [HBM] * 5,
        out_specs=(VMEM,) * 3,
        scratch_shapes=[
            field, pltpu.VMEM((STEPS, 2, CY + 2, SUB, LANES), F32), pltpu.VMEM((STEPS, 2, CZ, SUB, LANES), F32),
            face_z, face_y, face_z, face_y,
            picked, picked, pltpu.VMEM((CAP, LANES), F32),
            pltpu.SMEM((SLOTS,), I32), count_s, pltpu.VMEM((TILES, CAP), I32), pltpu.VMEM((TILES, 1, CAP), I32),
            pltpu.VMEM((STEPS, SLOTS, K), BF16),
            pltpu.VMEM((HALVES, TILES, CAP, WIDE), BF16), pltpu.VMEM((HALVES, TILES, CAP, WIDE), BF16),
            pltpu.VMEM((TILES, 1, CAP), I32), pltpu.VMEM((TILES, OWN, CAP), BF16),
            pltpu.VMEM((HALVES, OWN, WIDE), F32), pltpu.VMEM((HALVES, SLABS, PART, WIDE), F32),
            pltpu.VMEM((HALVES, OWN, WIDE), BF16),
            DMA((5,)), DMA((STEPS, 8)), DMA((STEPS, 8)),
            DMA((TILES,)), DMA((TILES,)), DMA((HALVES, TILES)), DMA((HALVES, TILES)),
            DMA((HALVES, SLABS)), DMA((HALVES, SLABS)), DMA((HALVES, SLABS)), DMA((HALVES, SLABS)),
        ],
        compiler_params=pltpu.CompilerParams(
            vmem_limit_bytes=20 * MIB, collective_id=0, has_side_effects=True
        ),
        name="wave",
    )(
        *in_vmem(lam0, before, cour, keep),
        *in_hbm(wall_cell, block_count, cells, wall_patch.reshape(TILES, 1, CAP), history),
    )
    whole = jax.ShapeDtypeStruct((CZ, CY, NX), F32)
    gradient, final, previous = pl.pallas_call(
        write_kernel,
        out_shape=(jax.ShapeDtypeStruct((OWN, K), F32), whole, whole),
        in_specs=[VMEM] * 3,
        out_specs=(HBM,) * 3,
        scratch_shapes=[DMA((2, SUB)), DMA],
        compiler_params=pltpu.CompilerParams(vmem_limit_bytes=MIB),
        name="write",
    )(*in_vmem(lam2, lam3, result))
    return gradient, final, previous


def solution(mesh):
    return jax.shard_map(
        on_device,
        mesh=mesh,
        in_specs=(
            P("slab", "tile", None),
            P("slab", "tile", None),
            P("slab", "tile", None),
            P(("slab", "tile")),
            P(("slab", "tile")),
            P(("slab", "tile")),
            P(("slab", "tile")),
            P(None, ("slab", "tile"), None),
        ),
        out_specs=(P("tile", None), P("slab", "tile", None), P("slab", "tile", None)),
        check_vma=False,
    )
```
